512 devices in a mesh: clip: 4 (over x), vseq: 32 (over y, z_lo), aseq: 4 (over z_hi, core).
Axes of the slice: x: 4, y: 4, z: 16 (z_hi: 2, z_lo: 8; z = z_hi * 8 + z_lo), core: 2. Of those that a mesh axis runs over, the one named last changes fastest.
Arguments:
- video_q: bfloat16 [98304, 1536], P(('clip', 'vseq'), 'aseq'), parts along dimension 0, may hold values from -9 to 9
- video_k: bfloat16 [98304, 1536], P(('clip', 'vseq'), 'aseq'), parts along dimension 0, may hold values from -9 to 9
- video_v: bfloat16 [98304, 1536], P(('clip', 'vseq'), 'aseq'), parts along dimension 0, may hold values from -6 to 6
- audio_q: bfloat16 [2048, 1536], P(('clip', 'vseq'), 'aseq'), parts along dimension 0, may hold values from -9 to 9
- audio_k: bfloat16 [2048, 1536], P(('clip', 'vseq'), 'aseq'), parts along dimension 0, may hold values from -9 to 9
- audio_v: bfloat16 [2048, 1536], P(('clip', 'vseq'), 'aseq'), parts along dimension 0, may hold values from -6 to 6
- video_cot: bfloat16 [98304, 1536], P(('clip', 'vseq'), 'aseq'), parts along dimension 0, may hold values from -6 to 6
- audio_cot: bfloat16 [2048, 1536], P(('clip', 'vseq'), 'aseq'), parts along dimension 0, may hold values from -6 to 6
Outputs:
- video_out: bfloat16 [98304, 1536], P(('clip', 'vseq'), 'aseq'), parts along dimension 0
- audio_out: bfloat16 [2048, 1536], P(('clip', 'vseq'), 'aseq'), parts along dimension 0
- video_q_grad: bfloat16 [98304, 1536], P(('clip', 'vseq'), 'aseq'), parts along dimension 0
- video_k_grad: bfloat16 [98304, 1536], P(('clip', 'vseq'), 'aseq'), parts along dimension 0
- video_v_grad: bfloat16 [98304, 1536], P(('clip', 'vseq'), 'aseq'), parts along dimension 0
- audio_q_grad: bfloat16 [2048, 1536], P(('clip', 'vseq'), 'aseq'), parts along dimension 0
- audio_k_grad: bfloat16 [2048, 1536], P(('clip', 'vseq'), 'aseq'), parts along dimension 0
- audio_v_grad: bfloat16 [2048, 1536], P(('clip', 'vseq'), 'aseq'), parts along dimension 0
The draws below stay inside these ranges and needn't reach their ends.
There are 4 independent parts, one for each index of `clip`. The reference program is written for one: setup_inputs(seed, part) draws one part's arguments, and reference() takes and returns one part's arrays. A program takes and returns all parts, laid end to end along the dimension named above; each array names one. Nothing has to cross between parts.
All inputs are finite; a program needn't handle non-finite values.
Results may differ from the reference program's by a relative error of at most 0.02005.
Values may be sent and summed in bfloat16 or wider, within the bound.
No kernel may reach another device: no remote copies, remote signals or barrier semaphores. Data moves between devices by JAX's collectives and lax.ppermute only.
A program may use at most 64 MiB of HBM per device.

```python
import math
import jax
import jax.numpy as jnp
from jax import lax

HEADS = 12
HDIM = 128
VTOK = 24576
ATOK = 512


def drawn_rows(key, rows, spread, limit):
    return jnp.clip(spread * jax.random.normal(key, (rows, HEADS * HDIM), jnp.float32), -limit, limit)


def draw_video_q(key, part):
    key = jax.random.fold_in(key, 1)
    return drawn_rows(key, VTOK, 1.6, 8.0).astype(jnp.bfloat16)


def draw_audio_k(key, part):
    key = jax.random.fold_in(key, 2)
    return drawn_rows(key, ATOK, 1.6, 8.0).astype(jnp.bfloat16)


def draw_audio_q(key, part):
    key = jax.random.fold_in(key, 3)
    return drawn_rows(key, ATOK, 1.6, 8.0).astype(jnp.bfloat16)


def draw_video_k(key, part):
    key = jax.random.fold_in(key, 4)
    return drawn_rows(key, VTOK, 1.6, 8.0).astype(jnp.bfloat16)


def levels(key, shape, cuts, least, top_value):
    gain, own = 1.0, jax.random.fold_in(key, 6)
    for axis_at, parts in cuts:
        draws = jnp.exp(jax.random.uniform(jax.random.fold_in(own, axis_at), (parts,), jnp.float32, least / len(cuts), top_value / len(cuts)))
        gain = gain * jnp.repeat(draws, shape[axis_at] // parts).reshape([-1 if axis == axis_at else 1 for axis in range(len(shape))])
    return gain


def centred(own_key, shape, scale, most, pieces=(), dtype=jnp.bfloat16):
    values = jax.random.normal(own_key, shape, jnp.float32) * scale
    if len(pieces) > 0:
        values = levels(own_key, shape, pieces, -0.22, 0.18) * values
    return jnp.clip(values, min=-most, max=most).astype(dtype)


def setup_inputs(seed: int = 0, part: int = 0) -> dict:
    key_list = jax.random.split(jax.random.key(seed), 9)
    part_splits = jax.random.split(jax.random.fold_in(key_list[8], part), 9)
    video_q = draw_video_q(jax.random.fold_in(jax.random.fold_in(key_list[8], part), 71), part)
    video_k = draw_video_k(jax.random.fold_in(jax.random.fold_in(key_list[8], part), 71), part)
    video_v = centred(part_splits[2], (VTOK, HEADS * HDIM), 1.0, 6.0, ((0, 32), (1, 4)))
    audio_q = draw_audio_q(jax.random.fold_in(jax.random.fold_in(key_list[8], part), 71), part)
    audio_k = draw_audio_k(jax.random.fold_in(jax.random.fold_in(key_list[8], part), 71), part)
    audio_v = centred(part_splits[5], (ATOK, HEADS * HDIM), 1.0, 6.0, ((0, 32), (1, 4)))
    video_cot = centred(part_splits[6], (VTOK, HEADS * HDIM), 1.0, 6.0, ((0, 32), (1, 4)))
    audio_cot = centred(part_splits[7], (ATOK, HEADS * HDIM), 1.0, 6.0, ((0, 32), (1, 4)))
    return {"video_q": video_q, "video_k": video_k, "video_v": video_v, "audio_q": audio_q, "audio_k": audio_k, "audio_v": audio_v, "video_cot": video_cot, "audio_cot": audio_cot}


def one_head(operands):
    queries, key_rows, value_rows, cotangent = operands
    factor = 1.0 / math.sqrt(HDIM)
    scores = jnp.dot(queries, key_rows.T, preferred_element_type=jnp.float32) * factor
    row_peak = lax.optimization_barrier(jnp.max(scores, axis=1, keepdims=True))
    logsum = row_peak + jnp.log(lax.optimization_barrier(jnp.sum(jnp.exp(scores - row_peak), axis=1, keepdims=True)))
    weights = jnp.exp(scores - logsum).astype(jnp.bfloat16)
    output = jnp.dot(weights, value_rows, preferred_element_type=jnp.float32).astype(jnp.bfloat16)
    row_delta = lax.optimization_barrier(jnp.sum(cotangent.astype(jnp.float32) * output.astype(jnp.float32), axis=1, keepdims=True))
    dweights = jnp.dot(cotangent, value_rows.T, preferred_element_type=jnp.float32)
    grad_scores = (weights.astype(jnp.float32) * (dweights - row_delta) * factor).astype(jnp.bfloat16)
    query_grad = jnp.dot(grad_scores, key_rows, preferred_element_type=jnp.float32).astype(jnp.bfloat16)
    key_grad = jnp.dot(grad_scores.T, queries, preferred_element_type=jnp.float32).astype(jnp.bfloat16)
    value_grad = jnp.dot(weights.T, cotangent, preferred_element_type=jnp.float32).astype(jnp.bfloat16)
    return (output, query_grad, key_grad, value_grad)

def split_heads(matrix):
    return matrix.reshape(matrix.shape[0], HEADS, HDIM).transpose(1, 0, 2)

def join_heads(stacked):
    return stacked.transpose(1, 0, 2).reshape(stacked.shape[1], HEADS * HDIM)

def attend(queries, key_rows, value_rows, cotangent):
    results = lax.map(one_head, (split_heads(queries), split_heads(key_rows), split_heads(value_rows), split_heads(cotangent)))
    return tuple((join_heads(stacked) for stacked in results))

def reference(video_q, video_k, video_v, audio_q, audio_k, audio_v, video_cot, audio_cot):
    video_out, video_q_grad, audio_k_grad, audio_v_grad = attend(video_q, audio_k, audio_v, video_cot)
    audio_out, audio_q_grad, video_k_grad, video_v_grad = attend(audio_q, video_k, video_v, audio_cot)
    return (video_out, audio_out, video_q_grad, video_k_grad, video_v_grad, audio_q_grad, audio_k_grad, audio_v_grad)
```

```python
import functools
import math

import jax
import jax.numpy as jnp
from jax import lax
from jax.experimental import pallas as pl
from jax.experimental.pallas import tpu as pltpu
from jax.sharding import PartitionSpec as P

HDIM = 128
YS, ZS = 4, 8
SCALE = 1.0 / math.sqrt(HDIM)
SCALE2 = SCALE / math.log(2.0)
F32, BF16 = jnp.float32, jnp.bfloat16


def z_swap(d):
    return [(y * ZS + z, y * ZS + (z ^ d)) for y in range(YS) for z in range(ZS)]


def y_shift(j):
    return [(y * ZS + z, ((y + j) % YS) * ZS + z) for y in range(YS) for z in range(ZS)]


def gather_rows(block):
    for d in (4, 2, 1):
        block = jnp.concatenate([block, lax.ppermute(block, "vseq", z_swap(d))], axis=0)
    return [block] + [lax.ppermute(block, "vseq", y_shift(-j)) for j in range(1, YS)]


def scatter_rows(own, others):
    total = own
    for j in range(1, YS):
        total = total + lax.ppermute(others[j - 1], "vseq", y_shift(j)).astype(F32)
    for d in (1, 2, 4):
        half = total.shape[0] // 2
        got = lax.ppermute(total[half:].astype(BF16), "vseq", z_swap(d))
        total = total[:half] + got.astype(F32)
    return total


def nt(a, b):
    return lax.dot_general(a, b, (((1,), (1,)), ((), ())), preferred_element_type=F32)


def nn(a, b):
    return lax.dot_general(a, b, (((1,), (0,)), ((), ())), preferred_element_type=F32)


def joined(refs):
    return jnp.concatenate([ref[...] for ref in refs], axis=0)


def put_pieces(own_ref, other_refs, left, right):
    rows = own_ref.shape[0]
    for j, ref in enumerate([own_ref] + list(other_refs)):
        cut = slice(j * rows, (j + 1) * rows)
        ref[:, :HDIM] = left[:, cut].T.astype(ref.dtype)
        ref[:, HDIM:] = right[:, cut].T.astype(ref.dtype)


def video_kernel(chunk, q_ref, cot_ref, *refs):
    keys, values = joined(refs[0:4]), joined(refs[4:8])
    out_ref, qgrad_ref, own_ref = refs[8:11]
    key_sum = value_sum = None
    for at in range(0, q_ref.shape[0], chunk):
        rows = pl.ds(at, chunk)
        q, cot = q_ref[rows, :], cot_ref[rows, :]
        scores = nt(q, keys)
        peak = jnp.max(scores, axis=1, keepdims=True)
        e = jnp.exp2((scores - peak) * SCALE2)
        p = e * (1.0 / jnp.sum(e, axis=1, keepdims=True))
        pb = p.astype(BF16)
        out = nn(pb, values).astype(BF16)
        out_ref[rows, :] = out
        delta = jnp.sum(cot.astype(F32) * out.astype(F32), axis=1, keepdims=True)
        ds = (p * (nt(cot, values) - delta)).astype(BF16)
        qgrad_ref[rows, :] = (nn(ds, keys) * SCALE).astype(BF16)
        key_part, value_part = nn(q.T, ds), nn(cot.T, pb)
        key_sum = key_part if key_sum is None else key_sum + key_part
        value_sum = value_part if value_sum is None else value_sum + value_part
    put_pieces(own_ref, refs[11:14], key_sum * SCALE, value_sum)


def stats_kernel(chunk, k_ref, v_ref, *refs):
    queries, cots = joined(refs[0:4]), joined(refs[4:8])
    stats_ref, s_ref = refs[8:10]
    peak = None
    for at in range(0, k_ref.shape[0], chunk):
        rows = pl.ds(at, chunk)
        scores = nt(k_ref[rows, :], queries) * SCALE2
        s_ref[rows, :] = scores
        top = jnp.max(scores, axis=0, keepdims=True)
        peak = top if peak is None else jnp.maximum(peak, top)
    total = weighted = jnp.zeros_like(peak)
    for at in range(0, k_ref.shape[0], chunk):
        rows = pl.ds(at, chunk)
        e = jnp.exp2(s_ref[rows, :] - peak)
        total = total + jnp.sum(e, axis=0, keepdims=True)
        weighted = weighted + jnp.sum(e * nt(v_ref[rows, :], cots), axis=0, keepdims=True)
    stats_ref[0, 0:1, :] = peak
    stats_ref[0, 1:2, :] = total
    stats_ref[0, 2:3, :] = weighted
    stats_ref[0, 3:8, :] = jnp.zeros((5, peak.shape[1]), F32)


def swapped(x, d):
    if d == 0:
        return x
    width = x.shape[1] // YS
    size = (width // ZS) * {4: 1, 2: 2, 1: 4}[d]
    parts = [x[:, at : at + size] for at in range(0, x.shape[1], size)]
    return jnp.concatenate([parts[i ^ 1] for i in range(len(parts))], axis=1)


def turned(x, j):
    width = x.shape[1] // YS
    parts = [x[:, i * width : (i + 1) * width] for i in range(YS)]
    return jnp.concatenate([parts[(i + j) % YS] for i in range(YS)], axis=1)


def merge_kernel(d, own_ref, *refs):
    merged_ref = refs[-1]
    for head in range(own_ref.shape[0]):
        terms = [own_ref[head]]
        for j, ref in enumerate(refs[:-1]):
            terms.append(swapped(ref[head], d) if d else turned(ref[head], j + 1))
        peak = functools.reduce(jnp.maximum, [t[0:1] for t in terms])
        merged_ref[head] = jnp.concatenate(
            [peak, sum(t[1:] * jnp.exp2(t[0:1] - peak) for t in terms)], axis=0
        )


def merge(d, own, others):
    return pl.pallas_call(
        functools.partial(merge_kernel, d),
        out_shape=jax.ShapeDtypeStruct(own.shape, F32),
    )(own, *others)


def audio_kernel(chunk, stats_ref, k_ref, v_ref, *refs):
    queries, cots = joined(refs[0:4]), joined(refs[4:8])
    kgrad_ref, vgrad_ref, own_ref = refs[8:11]
    logsum = stats_ref[0, 0:1, :] + jnp.log2(stats_ref[0, 1:2, :])
    delta = stats_ref[0, 2:3, :] / stats_ref[0, 1:2, :]
    out_sum = query_sum = None
    for at in range(0, k_ref.shape[0], chunk):
        rows = pl.ds(at, chunk)
        k, v = k_ref[rows, :], v_ref[rows, :]
        p = jnp.exp2(nt(k, queries) * SCALE2 - logsum)
        pb = p.astype(BF16)
        ds = (p * (nt(v, cots) - delta)).astype(BF16)
        vgrad_ref[rows, :] = nn(pb, cots).astype(BF16)
        kgrad_ref[rows, :] = (nn(ds, queries) * SCALE).astype(BF16)
        out_part, query_part = nn(v.T, pb), nn(k.T, ds)
        out_sum = out_part if out_sum is None else out_sum + out_part
        query_sum = query_part if query_sum is None else query_sum + query_part
    put_pieces(own_ref, refs[11:14], out_sum, query_sum * SCALE)


def specs(video_rows, piece_rows, heads):
    by_head = pl.BlockSpec((video_rows, HDIM), lambda h: (0, h))
    first = [pl.BlockSpec((piece_rows, HDIM), lambda h: (0, h))] * YS
    second = [pl.BlockSpec((piece_rows, HDIM), lambda h: (0, heads + h))] * YS
    sums = [pl.BlockSpec((piece_rows, 2 * HDIM), lambda h: (0, h))] * YS
    return by_head, first + second, sums


def piece_shapes(piece_rows, heads):
    return [
        jax.ShapeDtypeStruct((piece_rows, heads * 2 * HDIM), F32 if j == 0 else BF16)
        for j in range(YS)
    ]


PARAMS = pltpu.CompilerParams(vmem_limit_bytes=40 * 1024 * 1024)


def unpaired(pairs):
    both = pairs.reshape(pairs.shape[0], -1, 2, HDIM)
    return [both[:, :, i].reshape(pairs.shape[0], -1).astype(BF16) for i in range(2)]


def body(video_q, video_k, video_v, audio_q, audio_k, audio_v, video_cot, audio_cot):
    rows, cols = video_q.shape
    heads = cols // HDIM
    chunk = math.gcd(rows, 256)
    audio_rows = audio_q.shape[0] * YS * ZS
    query_pieces = gather_rows(jnp.concatenate([audio_q, audio_cot], axis=1))
    key_pieces = gather_rows(jnp.concatenate([audio_k, audio_v], axis=1))
    by_head, piece_specs, sum_specs = specs(rows, audio_rows // YS, heads)
    stats_spec = pl.BlockSpec((1, 8, audio_rows), lambda h: (h, 0, 0))
    like = jax.ShapeDtypeStruct((rows, cols), BF16)
    pieces = piece_shapes(audio_rows // YS, heads)

    stats = pl.pallas_call(
        functools.partial(stats_kernel, chunk),
        grid=(heads,),
        in_specs=[by_head] * 2 + piece_specs,
        out_specs=stats_spec,
        out_shape=jax.ShapeDtypeStruct((heads, 8, audio_rows), F32),
        scratch_shapes=[pltpu.VMEM((rows, audio_rows), F32)],
        compiler_params=PARAMS,
        name="audio_stats",
    )(video_k, video_v, *query_pieces, *query_pieces)
    stats = merge(0, stats, [lax.ppermute(stats, "vseq", y_shift(j)) for j in range(1, YS)])
    for d in (1, 2, 4):
        stats = merge(d, stats, [lax.ppermute(stats, "vseq", z_swap(d))])

    video_out, video_q_grad, *key_sums = pl.pallas_call(
        functools.partial(video_kernel, chunk),
        grid=(heads,),
        in_specs=[by_head] * 2 + piece_specs,
        out_specs=[by_head] * 2 + sum_specs,
        out_shape=[like] * 2 + pieces,
        compiler_params=PARAMS,
        name="video_queries",
    )(video_q, video_cot, *key_pieces, *key_pieces)
    audio_k_grad, audio_v_grad = unpaired(scatter_rows(key_sums[0], key_sums[1:]))

    video_k_grad, video_v_grad, *query_sums = pl.pallas_call(
        functools.partial(audio_kernel, chunk),
        grid=(heads,),
        in_specs=[stats_spec] + [by_head] * 2 + piece_specs,
        out_specs=[by_head] * 2 + sum_specs,
        out_shape=[like] * 2 + pieces,
        compiler_params=PARAMS,
        name="audio_queries",
    )(stats, video_k, video_v, *query_pieces, *query_pieces)
    audio_out, audio_q_grad = unpaired(scatter_rows(query_sums[0], query_sums[1:]))
    return (
        video_out,
        audio_out,
        video_q_grad,
        video_k_grad,
        video_v_grad,
        audio_q_grad,
        audio_k_grad,
        audio_v_grad,
    )


def solution(mesh):
    placed = (P(("clip", "vseq"), "aseq"),) * 8
    return jax.shard_map(body, mesh=mesh, in_specs=placed, out_specs=placed, check_vma=False)
```
